256 devices in a mesh: freq: 64 (over z, y, core), col: 4 (over x).
Axes of the slice: x: 4, y: 4, z: 8, core: 2. Of those that a mesh axis runs over, the one named last changes fastest.
Arguments:
- traces: bfloat16 [16, 512, 64, 512], P('col', 'freq'), may hold values from -6 to 6
- left_factors: bfloat16 [256, 16, 16, 16, 512], P('freq', None, 'col'), may hold values from -0.5 to 0.5
- right_factors: bfloat16 [256, 16, 16, 16, 512], P('freq', None, 'col'), may hold values from -0.25 to 0.25
- tile_ranks: int32 [256, 16, 16], P('freq', None, 'col'), may hold values from 1 to 16, as said below
Outputs:
- modelled: bfloat16 [16, 512, 64, 512], P('col', 'freq')
The draws below stay inside these ranges and needn't reach their ends.
Inputs may be any that keep to these rules, and one draw needn't show every extreme that they name: `tile_ranks`: the rank of each kernel tile; factor rows at or past it are not part of the kernel. 16 is reached by some tile in every draw.
All inputs are finite; a program needn't handle non-finite values.
Results may differ from the reference program's by a relative error of at most 0.0072.
Values may be sent and summed in bfloat16 or wider, within the bound.
A program may use at most 128 MiB of HBM per device.

```python
import jax
import jax.numpy as jnp
from jax import lax

NT = 512
TS = 512
RMAX = 16
NF = 256
NVB = 64
RT = 16
CT = 16


def draw_tile_ranks(key, part):
    base_key = jax.random.fold_in(key, 11)
    first_key, second_key, third_key = jax.random.split(base_key, 3)
    freq_index = jnp.arange(NF, dtype=jnp.int32)[:, None, None]
    low_cap = max(RMAX // 4, 1)
    rank_caps = low_cap + (RMAX - low_cap) * freq_index // max(NF - 1, 1)
    raw_draws = jax.random.randint(first_key, (NF, RT, CT), 0, 1 << 20)
    ranks_drawn = 1 + raw_draws % rank_caps
    chosen_freq = jax.random.randint(second_key, (), NF // 2, NF)
    chosen_tile = jax.random.randint(third_key, (), 0, RT * CT)
    tile_index = jnp.arange(RT * CT, dtype=jnp.int32).reshape(1, RT, CT)
    chosen_mask = (freq_index == chosen_freq) & (tile_index == chosen_tile)
    return jnp.where(chosen_mask, RMAX, ranks_drawn).astype(jnp.int32)


def strengthened(values, stream_key, source, target, parts, factor):
    owner, partner = [(jnp.arange(values.shape[position]) // (values.shape[position] // parts)).reshape([-1 if axis == position else 1 for axis in range(values.ndim)]) for position in (source, target)]
    chosen = jax.random.permutation(stream_key, parts)[partner]
    strong = (owner == chosen) | (owner == (partner + parts // 2) % parts)
    return jnp.where(strong, factor * values, values)


def shard_levels(stream_key, extent, pieces, least, high):
    level = 1.0
    for position, blocks in pieces:
        steps = jax.random.uniform(jax.random.fold_in(jax.random.fold_in(stream_key, 6), position), (blocks,), jnp.float32, least / len(pieces), high / len(pieces))
        level = level * jnp.repeat(jnp.exp(steps), extent[position] // blocks).reshape((-1,) + (1,) * (len(extent) - 1 - position))
    return level


def normal_values(stream_key, shape, spread, limit, cuts=(), held_as=jnp.bfloat16):
    level = shard_levels(stream_key, shape, cuts, -0.22, 0.18) if cuts else 1.0
    drawn = jax.random.normal(stream_key, shape, jnp.float32) * spread * level
    return jnp.minimum(jnp.maximum(drawn, -limit), limit).astype(held_as)


def noise_with(key, dims, spread, limit, shards, heavy, kind=jnp.bfloat16):
    array = spread * jax.random.normal(key, dims, jnp.float32)
    if shards:
        array = array * shard_levels(key, dims, shards, -0.22, 0.18)
    return jnp.clip(strengthened(array, jax.random.fold_in(key, 3), *heavy), -limit, limit).astype(kind)


def setup_inputs(seed: int = 0) -> dict:
    keys = jax.random.split(jax.random.key(seed), 5)
    return {
        "traces": normal_values(keys[0], (CT, TS, NVB, NT), 1.0, 6.0, ((0, 4), (1, 64))),
        "left_factors": noise_with(keys[1], (NF, RT, CT, RMAX, TS), (RMAX * CT) ** -0.5, 0.5, ((0, 64), (2, 4)), (2, 1, 4, 2.0)),
        "right_factors": normal_values(keys[2], (NF, RT, CT, RMAX, TS), TS ** -0.5, 0.25, ((0, 64), (2, 4))),
        "tile_ranks": draw_tile_ranks(jax.random.fold_in(keys[4], 71), 0),
    }


def hartley_table(time_count, freq_count):
    times = jnp.arange(time_count, dtype=jnp.int32)
    freqs = jnp.arange(freq_count, dtype=jnp.int32)
    phase = times[:, None] * freqs[None, :] % time_count
    angle = 2.0 * jnp.pi / time_count * phase.astype(jnp.float32)
    scale = jnp.sqrt(jnp.float32(time_count))
    return ((jnp.cos(angle) + jnp.sin(angle)) / scale).astype(jnp.bfloat16)

def reference(traces, left_factors, right_factors, tile_ranks):
    cas_table = hartley_table(NT, NF).astype(jnp.float32)

    def forward(tile):
        return jnp.einsum('swt,tk->kws', tile.astype(jnp.float32), cas_table).astype(jnp.bfloat16)
    spectra = jnp.moveaxis(lax.map(forward, traces), 1, 0)

    def apply_kernel(operands):
        spectrum, right_tiles, left_tiles, rank_tiles = operands
        coeffs = jnp.einsum('cws,rcks->rwck', spectrum.astype(jnp.float32), right_tiles.astype(jnp.float32))
        kept_mask = jnp.arange(RMAX, dtype=jnp.int32)[None, None, None, :] < rank_tiles[:, None, :, None]
        coeffs = jnp.where(kept_mask, coeffs, jnp.float32(0.0)).astype(jnp.bfloat16)
        summed = jnp.einsum('rwck,rcks->rws', coeffs.astype(jnp.float32), left_tiles.astype(jnp.float32))
        return summed.astype(jnp.bfloat16)
    synthesis = lax.map(apply_kernel, (spectra, right_factors, left_factors, tile_ranks))
    synthesis = jnp.moveaxis(synthesis, 1, 0)

    def inverse(block):
        return jnp.einsum('kws,tk->swt', block.astype(jnp.float32), cas_table).astype(jnp.bfloat16)
    return lax.map(inverse, synthesis)
```

```python
import jax
import jax.numpy as jnp
import numpy as np
from jax import lax
from jax.experimental import pallas as pl
from jax.experimental.pallas import tpu as pltpu
from jax.sharding import PartitionSpec as P

MESH = pl.DeviceIdType.MESH
F32, BF16 = jnp.float32, jnp.bfloat16
NZ, NY, NC, NX = 8, 4, 2, 4
NFREQ = NZ * NY * NC
KL = 4


def hartley_rows(time_count, freq_count):
    phase = np.arange(freq_count)[:, None] * np.arange(time_count)[None, :] % time_count
    angle = np.float32(2.0 * np.pi / time_count) * phase.astype(np.float32)
    table = (np.cos(angle) + np.sin(angle)) / np.sqrt(np.float32(time_count))
    return jnp.asarray(table.astype(np.float32)).astype(BF16)


def freq_peer(f, i):
    z, y, c = f // (NY * NC), lax.rem(f // NC, NY), lax.rem(f, NC)
    dz, dy, dc = lax.rem(i, NZ), lax.rem(i // NZ, NY), i // (NZ * NY)
    return (lax.rem(z + dz, NZ) * NY + lax.rem(y + dy, NY)) * NC + lax.rem(c + dc, NC)


def kernel(
    cas, ranks, traces, left, right, out,
    tr, rt, lall, stage, send, recv, csend, crecv, send2, recv2, stage2, outv,
    local_sem, spec_sem, left_sem, coef_sem, syn_sem, out_sem,
):
    f, x = lax.axis_index("freq"), lax.axis_index("col")

    def spec_copy(i, k):
        d = freq_peer(f, i)
        return pltpu.make_async_remote_copy(
            send.at[d, k], recv.at[f, k], spec_sem.at[0, k], spec_sem.at[1, k],
            device_id=(d, x), device_id_type=MESH,
        )

    def syn_copy(i, k):
        d = freq_peer(f, i)
        return pltpu.make_async_remote_copy(
            send2.at[d, k], recv2.at[f, k], syn_sem.at[0, k], syn_sem.at[1, k],
            device_id=(d, x), device_id_type=MESH,
        )

    def left_copy(o, k):
        d = lax.rem(x + o, NX)
        return pltpu.make_async_remote_copy(
            left.at[k, pl.ds(4 * d, 4)], lall.at[k, :, x], left_sem.at[0, k], left_sem.at[1, k],
            device_id=(f, d), device_id_type=MESH,
        )

    def coef_copy(o, k):
        d = lax.rem(x + o, NX)
        return pltpu.make_async_remote_copy(
            csend.at[k, d], crecv.at[k, x], coef_sem.at[0, k], coef_sem.at[1, k],
            device_id=(f, d), device_id_type=MESH,
        )

    def whole(src, dst, sems, k):
        return pltpu.make_async_remote_copy(
            src, dst, sems.at[0, k], sems.at[1, k], device_id=(f, x), device_id_type=MESH
        )

    rest = pl.ds(0, NFREQ - 1)

    def spec_all(k):
        return whole(send.at[rest, k], recv.at[rest, k], spec_sem, k)

    def syn_all(k):
        return whole(send2.at[rest, k], recv2.at[rest, k], syn_sem, k)

    def left_all(k):
        return whole(left.at[k, pl.ds(0, 12)], lall.at[k, :, pl.ds(0, 3)], left_sem, k)

    def coef_all(k):
        return whole(csend.at[k, pl.ds(0, 3)], crecv.at[k, pl.ds(0, 3)], coef_sem, k)

    barrier = pltpu.get_barrier_semaphore()

    def greet(i, carry):
        pl.semaphore_signal(
            barrier, inc=1, device_id=(freq_peer(f, i), x), device_id_type=MESH
        )
        return carry

    lax.fori_loop(1, NFREQ, greet, 0)
    for o in range(1, NX):
        pl.semaphore_signal(
            barrier, inc=1, device_id=(f, lax.rem(x + o, NX)), device_id_type=MESH
        )

    traces_in = pltpu.make_async_copy(traces, tr, local_sem.at[0])
    right_in = pltpu.make_async_copy(right, rt, local_sem.at[1])
    left_in = pltpu.make_async_copy(left.at[:, pl.ds(4 * x, 4)], lall.at[:, :, x], local_sem.at[2])
    traces_in.start()
    right_in.start()
    left_in.start()

    pl.semaphore_wait(barrier, NFREQ - 1 + NX - 1)
    for k in range(KL):
        for o in (1, 3, 2):
            left_copy(o, k).start()

    traces_in.wait()

    def spectra(n, carry):
        p, s = n // 8, lax.rem(n, 8)
        rows = jnp.concatenate([tr[2 * p, s], tr[2 * p + 1, s]], axis=0)
        acc = lax.dot_general(
            cas[...], rows, (((1,), (1,)), ((), ())), preferred_element_type=F32
        )
        stage[p, pl.ds(s, 256, 8), :] = acc
        return carry

    lax.fori_loop(0, 16, spectra, 0)

    def pack(n, carry):
        halves = [stage[p, pl.ds(n * 256, 256), :].reshape(8, KL, 8, 128) for p in range(2)]
        send[pl.ds(n * 8, 8)] = jnp.concatenate(halves, axis=2).astype(BF16)
        return carry

    lax.fori_loop(0, 8, pack, 0)

    def start_spec(n, carry):
        k, i = n // NFREQ, lax.rem(n, NFREQ)

        @pl.when(i > 0)
        def _():
            spec_copy(i, k).start()

        return carry

    lax.fori_loop(0, KL * NFREQ, start_spec, 0)
    recv[pl.ds(f, 1)] = send[pl.ds(f, 1)]
    right_in.wait()

    lane = lax.broadcasted_iota(jnp.int32, (256, 128), 1)
    rank_index = lax.rem(lax.broadcasted_iota(jnp.int32, (256, 128), 0), 16)

    def coeffs(k):
        spec_all(k).wait_recv()
        spectrum = recv[:, k].astype(F32)
        for p in range(2):
            rows = spectrum[:, 8 * p : 8 * p + 8].reshape(512, 128).astype(BF16)
            products = [
                jnp.dot(rt[k, :, 2 * p + b].reshape(256, 512), rows, preferred_element_type=F32)
                for b in range(2)
            ]
            limits = jnp.where(
                lax.broadcasted_iota(jnp.int32, (16, 128), 1) < 64,
                jnp.broadcast_to(ranks[k, :, 2 * p : 2 * p + 1], (16, 128)),
                jnp.broadcast_to(ranks[k, :, 2 * p + 1 : 2 * p + 2], (16, 128)),
            )
            limits = jnp.concatenate(
                [jnp.broadcast_to(limits[r : r + 1], (16, 128)) for r in range(16)], axis=0
            )
            kept = jnp.where(lane < 64, products[0], products[1])
            kept = jnp.where(rank_index < limits, kept, 0.0).astype(BF16)
            csend[k, :, p] = kept.reshape(4, 64, 128)
        crecv[k, pl.ds(x, 1)] = csend[k, pl.ds(x, 1)]
        for o in (1, 3, 2):
            coef_copy(o, k).start()

    def synthesis(k):
        coef_all(k).wait_recv()
        left_all(k).wait_recv()
        sums = []
        for r in range(4):
            mine = crecv[k, :, :, 16 * r : 16 * r + 16].reshape(128, 128)
            turned = mine.astype(F32).T.astype(BF16)
            lhs = jnp.concatenate([turned[:64], turned[64:]], axis=1)
            rhs = jnp.concatenate(
                [lall[k, r, :, :, b].reshape(128, 512) for b in range(2)], axis=0
            )
            sums.append(jnp.dot(lhs, rhs, preferred_element_type=F32))
        halves = [
            jnp.concatenate(sums[2 * q : 2 * q + 2], axis=0).T.reshape(64, 8, 128) for q in range(2)
        ]
        send2[:, k] = jnp.concatenate(halves, axis=1).astype(BF16)
        recv2[pl.ds(f, 1), k] = send2[pl.ds(f, 1), k]

        def start(i, carry):
            syn_copy(i, k).start()
            return carry

        lax.fori_loop(1, NFREQ, start, 0)

    coeffs(0)
    left_in.wait()

    def both(k, carry):
        coeffs(k + 1)
        synthesis(k)
        return carry

    lax.fori_loop(0, KL - 1, both, 0)
    synthesis(KL - 1)

    def gather(k, carry):
        syn_all(k).wait_recv()

        def one(n, inner):
            stage2[pl.ds(n * 64 + k * 16, 16), :] = recv2[n, k].astype(F32)
            return inner

        lax.fori_loop(0, NFREQ, one, 0, unroll=8)
        return carry

    lax.fori_loop(0, KL, gather, 0)

    def inverse(n, carry):
        q, s = n // 8, lax.rem(n, 8)
        rows = stage2[pl.ds(n, 256, 16), :].T.astype(BF16)
        acc = jnp.dot(rows, cas[...], preferred_element_type=F32).astype(BF16)
        outv[2 * q, s] = acc[:64]
        outv[2 * q + 1, s] = acc[64:]
        return carry

    out_copies = [
        pltpu.make_async_copy(outv.at[pl.ds(2 * q, 2)], out.at[pl.ds(2 * q, 2)], out_sem.at[q])
        for q in range(2)
    ]
    for q in range(2):
        lax.fori_loop(8 * q, 8 * q + 8, inverse, 0)
        out_copies[q].start()
    for k in range(KL):
        spec_all(k).wait_send()
        left_all(k).wait_send()
        coef_all(k).wait_send()
        syn_all(k).wait_send()
    for q in range(2):
        out_copies[q].wait()


def shards(traces, left_factors, right_factors, tile_ranks):
    cas = hartley_rows(512, 256)
    vmem = pl.BlockSpec(memory_space=pltpu.VMEM)
    hbm = pl.BlockSpec(memory_space=pl.ANY)
    return pl.pallas_call(
        kernel,
        out_shape=jax.ShapeDtypeStruct((4, 8, 64, 512), BF16),
        in_specs=[vmem, vmem, hbm, hbm, hbm],
        out_specs=hbm,
        scratch_shapes=[
            pltpu.VMEM((4, 8, 64, 512), BF16),
            pltpu.VMEM((4, 16, 4, 16, 512), BF16),
            pltpu.VMEM((4, 4, 4, 2, 2, 16, 512), BF16),
            pltpu.VMEM((2, 2048, 128), F32),
            pltpu.VMEM((64, 4, 16, 128), BF16),
            pltpu.VMEM((64, 4, 16, 128), BF16),
            pltpu.VMEM((4, 4, 2, 64, 128), BF16),
            pltpu.VMEM((4, 4, 2, 64, 128), BF16),
            pltpu.VMEM((64, 4, 16, 128), BF16),
            pltpu.VMEM((64, 4, 16, 128), BF16),
            pltpu.VMEM((4096, 128), F32),
            pltpu.VMEM((4, 8, 64, 512), BF16),
            pltpu.SemaphoreType.DMA((3,)),
            pltpu.SemaphoreType.DMA((2, KL)),
            pltpu.SemaphoreType.DMA((2, KL)),
            pltpu.SemaphoreType.DMA((2, KL)),
            pltpu.SemaphoreType.DMA((2, KL)),
            pltpu.SemaphoreType.DMA((2,)),
        ],
        compiler_params=pltpu.CompilerParams(
            collective_id=0, has_side_effects=True, vmem_limit_bytes=48 << 20
        ),
        cost_estimate=pl.CostEstimate(flops=2 * 10**9, bytes_accessed=16 << 20, transcendentals=0),
        name="tiles",
    )(
        cas,
        tile_ranks,
        traces,
        left_factors.reshape(4, 16, 2, 2, 16, 512),
        right_factors,
    )


def solution(mesh):
    in_specs = (
        P("col", "freq", None, None),
        P("freq", None, "col", None, None),
        P("freq", None, "col", None, None),
        P("freq", None, "col"),
    )
    out_specs = P("col", "freq", None, None)
    return jax.shard_map(shards, mesh=mesh, in_specs=in_specs, out_specs=out_specs, check_vma=False)
```

```python
import jax
import jax.numpy as jnp
import numpy as np
from jax import lax
from jax.experimental import pallas as pl
from jax.experimental.pallas import tpu as pltpu
from jax.sharding import PartitionSpec as P

MESH = pl.DeviceIdType.MESH
F32, BF16 = jnp.float32, jnp.bfloat16
NZ, NY, NC, NX = 8, 4, 2, 4
NFREQ = NZ * NY * NC
KL = 4
PART = 8


def hartley_rows(time_count, freq_count, stride=1):
    freqs = np.arange(freq_count).reshape(-1, stride).T.reshape(-1)
    phase = freqs[:, None] * np.arange(time_count)[None, :] % time_count
    angle = np.float32(2.0 * np.pi / time_count) * phase.astype(np.float32)
    table = (np.cos(angle) + np.sin(angle)) / np.sqrt(np.float32(time_count))
    return jnp.asarray(table.astype(np.float32)).astype(BF16)


def freq_peer(f, i):
    z, y, c = f // (NY * NC), lax.rem(f // NC, NY), lax.rem(f, NC)
    dz, dy, dc = lax.rem(i, NZ), lax.rem(i // NZ, NY), i // (NZ * NY)
    return (lax.rem(z + dz, NZ) * NY + lax.rem(y + dy, NY)) * NC + lax.rem(c + dc, NC)


def kernel(
    cas_in, ranks, traces, left, right, out,
    cas, limits, tr, rt, lloc, lrecv, hold, chain, stage, send, recv, csend, crecv, send2, recv2, stage2, turned_rows,
    local_sem, spec_sem, left_sem, coef_sem, chain_sem, syn_sem, out_sem,
):
    f, x = lax.axis_index("freq"), lax.axis_index("col")
    after, before, across = lax.rem(x + 1, NX), lax.rem(x + NX - 1, NX), lax.rem(x + 2, NX)
    routes = [(across, 0, after), (after, 1, after), (across, 1, before), (before, 0, before)]

    def spec_copy(i, k):
        d = freq_peer(f, i)
        return pltpu.make_async_remote_copy(
            send.at[d, k], recv.at[f, k], spec_sem.at[0, k], spec_sem.at[1, k],
            device_id=(d, x), device_id_type=MESH,
        )

    def syn_copy(i, k):
        d = freq_peer(f, i)
        return pltpu.make_async_remote_copy(
            send2.at[d, k], recv2.at[f, k], syn_sem.at[0, k], syn_sem.at[1, k],
            device_id=(d, x), device_id_type=MESH,
        )

    def left_copy(slot, k):
        owner, q, d = routes[slot]
        return pltpu.make_async_remote_copy(
            left.at[k, pl.ds(4 * owner + 2 * q, 2)], lrecv.at[k, slot],
            left_sem.at[0, k, slot], left_sem.at[1, k, slot],
            device_id=(f, d), device_id_type=MESH,
        )

    def coef_copy(slot, k):
        owner, q, d = routes[slot]
        return pltpu.make_async_remote_copy(
            csend.at[k, owner, q], crecv.at[k, slot],
            coef_sem.at[0, k, slot], coef_sem.at[1, k, slot],
            device_id=(f, d), device_id_type=MESH,
        )

    def chain_copy(q, k):
        return pltpu.make_async_remote_copy(
            chain.at[0, k, q], chain.at[1, k, q], chain_sem.at[0, k, q], chain_sem.at[1, k, q],
            device_id=(f, (after, before)[q]), device_id_type=MESH,
        )

    def whole(src, dst, sems, k):
        return pltpu.make_async_remote_copy(
            src, dst, sems.at[0, k], sems.at[1, k], device_id=(f, x), device_id_type=MESH
        )

    rest = pl.ds(0, NFREQ - 1)

    def spec_all(k):
        return whole(send.at[rest, k], recv.at[rest, k], spec_sem, k)

    def syn_all(k):
        return whole(send2.at[rest, k], recv2.at[rest, k], syn_sem, k)

    def far_left(k):
        left_copy(0, k).start()
        left_copy(2, k).start()

    def near_left(k):
        left_copy(1, k).start()
        left_copy(3, k).start()

    traces_in = pltpu.make_async_copy(traces, tr, local_sem.at[0])
    right_in = pltpu.make_async_copy(right, rt, local_sem.at[1])
    left_in = pltpu.make_async_copy(left, lloc, local_sem.at[2])
    cas_load = pltpu.make_async_copy(cas_in, cas, local_sem.at[3])
    traces_in.start()
    cas_load.start()
    right_in.start()
    left_in.start()

    barrier = pltpu.get_barrier_semaphore()

    def greet(i, carry):
        pl.semaphore_signal(
            barrier, inc=1, device_id=(freq_peer(f, i), x), device_id_type=MESH
        )
        return carry

    lax.fori_loop(1, NFREQ, greet, 0)
    for d in (after, before):
        pl.semaphore_signal(barrier, inc=1, device_id=(f, d), device_id_type=MESH)

    cas_load.wait()
    traces_in.wait()

    def spectra(n, carry):
        p, s = n // 4, 2 * lax.rem(n, 4)
        rows = jnp.concatenate(
            [tr[2 * p, s], tr[2 * p + 1, s], tr[2 * p, s + 1], tr[2 * p + 1, s + 1]], axis=0
        )
        acc = lax.dot_general(
            cas[...], rows, (((1,), (1,)), ((), ())), preferred_element_type=F32
        )
        stage[p, pl.ds(s, 256, 8), :] = acc[:, :128]
        stage[p, pl.ds(s + 1, 256, 8), :] = acc[:, 128:]
        return carry

    lax.fori_loop(0, 8, spectra, 0, unroll=2)

    def pack(n, carry):
        halves = [stage[p, pl.ds(n * 256, 256), :].reshape(8, KL, 8, 128) for p in range(2)]
        send[pl.ds(n * 8, 8)] = jnp.concatenate(halves, axis=2).astype(BF16)
        return carry

    lax.fori_loop(0, 8, pack, 0)

    row16 = lax.broadcasted_iota(jnp.int32, (16, 16), 0)
    diagonal = row16 == lax.broadcasted_iota(jnp.int32, (16, 16), 1)
    low_half = lax.broadcasted_iota(jnp.int32, (16, 128), 1) < 64
    for k in range(KL):
        for p in range(2):
            columns = [
                jnp.sum(
                    jnp.where(diagonal, ranks[k, 2 * p + b : 2 * p + b + 1].astype(F32), 0.0),
                    axis=1, keepdims=True,
                )
                for b in range(2)
            ]
            limits[k, p] = jnp.where(
                low_half, jnp.broadcast_to(columns[0], (16, 128)), jnp.broadcast_to(columns[1], (16, 128))
            )

    pl.semaphore_wait(barrier, NFREQ - 1 + 2)
    far_left(0)
    near_left(0)
    far_left(1)
    near_left(1)

    def start_spec(n, carry):
        k, i = n // NFREQ, lax.rem(n, NFREQ)

        @pl.when(i > 0)
        def _():
            spec_copy(i, k).start()

        return carry

    lax.fori_loop(0, KL * NFREQ, start_spec, 0)
    recv[pl.ds(f, 1)] = send[pl.ds(f, 1)]
    right_in.wait()

    lane = lax.broadcasted_iota(jnp.int32, (256, 128), 1)
    rank_index = lax.rem(lax.broadcasted_iota(jnp.int32, (256, 128), 0), 16).astype(F32)

    def coeffs(k):
        spec_all(k).wait_recv()
        spectrum = recv[:, k].astype(F32)
        for p in range(2):
            rows = spectrum[:, 8 * p : 8 * p + 8].reshape(512, 128).astype(BF16)
            products = [
                jnp.dot(rt[k, :, 2 * p + b].reshape(256, 512), rows, preferred_element_type=F32)
                for b in range(2)
            ]
            bound = jnp.concatenate(
                [jnp.broadcast_to(limits[k, p, r : r + 1], (16, 128)) for r in range(16)], axis=0
            )
            kept = jnp.where(lane < 64, products[0], products[1])
            kept = jnp.where(rank_index < bound, kept, 0.0).astype(BF16)
            csend[k, :, :, p] = kept.reshape(4, 2, 32, 128)
        for slot in (0, 2, 1, 3):
            coef_copy(slot, k).start()

    def spread(k, pairs):
        halves = [pair.T.reshape(64, 8, 128) for pair in pairs]
        send2[:, k] = jnp.concatenate(halves, axis=1).astype(BF16)
        recv2[pl.ds(f, 1), k] = send2[pl.ds(f, 1), k]

        def start(i, carry):
            syn_copy(i, k).start()
            return carry

        lax.fori_loop(1, NFREQ, start, 0)

    half = lax.broadcasted_iota(jnp.int32, (64, 256), 1) // 16 % 2

    def pair_sum(k, owner, q, slot):
        coefs = jnp.concatenate(
            [csend[k, owner, q].reshape(64, 128), crecv[k, slot].reshape(64, 128)], axis=0
        )
        turned = coefs.astype(F32).T
        lanes = jnp.concatenate([turned[:64], turned[64:]], axis=1)
        lhs = jnp.concatenate([jnp.where(half == r, lanes, 0.0) for r in range(2)], axis=0)
        rhs = []
        for b in range(2):
            rhs += [lloc[k, pl.ds(4 * owner + 2 * q, 2), p, b].reshape(32, 512) for p in range(2)]
            rhs += [lrecv[k, slot, :, p, b].reshape(32, 512) for p in range(2)]
        return jnp.dot(
            lhs.astype(BF16), jnp.concatenate(rhs, axis=0), preferred_element_type=F32
        )

    def arrived(k, slot):
        left_copy(slot, k).wait_recv()
        coef_copy(slot, k).wait_recv()

    def sums(k):
        arrived(k, 0)
        chain[0, k, 0] = pair_sum(k, after, 0, 0).astype(BF16)
        chain_copy(0, k).start()
        arrived(k, 2)
        chain[0, k, 1] = pair_sum(k, before, 1, 2).astype(BF16)
        chain_copy(1, k).start()

    def own_sums(k):
        arrived(k, 3)
        hold[k, 0] = pair_sum(k, x, 0, 3)
        arrived(k, 1)
        hold[k, 1] = pair_sum(k, x, 1, 1)

    def finish(k):
        for q in range(2):
            chain_copy(q, k).wait_recv()
        spread(k, [hold[k, q] + chain[1, k, q].astype(F32) for q in range(2)])

    steps = ["C0", "A2", "C1", "W", "X0", "B2", "Y0", "C2", "F0", "A3", "X1", "B3", "Y1", "C3", "F1", "X2", "X3", "Y2", "F2", "Y3", "F3"]
    for step in steps:
        if step == "W":
            left_in.wait()
            continue
        dict(C=coeffs, A=far_left, B=near_left, X=sums, Y=own_sums, F=finish)[step[0]](int(step[1]))

    def lanes_out(h):
        part = (slice(None), pl.ds(128 * h, 128))
        return pltpu.make_async_copy(turned_rows.at[part], out.at[part], out_sem.at[h])

    for k in range(KL):
        syn_all(k).wait_recv()
        stage2[...] = recv2[:, k].astype(F32).reshape(1024, 128)
        for n in range(16):
            turned_rows[128 * n : 128 * n + 128, 64 * k : 64 * k + 64] = (
                stage2[pl.ds(n, 64, 16), :].astype(BF16).T
            )

        if k % 2:
            lanes_out(k // 2).start()
    for k in range(KL):
        spec_all(k).wait_send()
        syn_all(k).wait_send()
        for slot in range(4):
            left_copy(slot, k).wait_send()
            coef_copy(slot, k).wait_send()
        for q in range(2):
            chain_copy(q, k).wait_send()
    for h in range(2):
        lanes_out(h).wait()


def inverse(rows, cas, out):
    acc = jnp.dot(rows[...], cas[...], preferred_element_type=F32).astype(BF16)
    for b in range(acc.shape[0] // 128):
        out[0, b] = acc[128 * b : 128 * b + 64]
        out[1, b] = acc[128 * b + 64 : 128 * b + 128]


def shards(traces, left_factors, right_factors, tile_ranks):
    cas = hartley_rows(512, 256)
    vmem = pl.BlockSpec(memory_space=pltpu.VMEM)
    hbm = pl.BlockSpec(memory_space=pl.ANY)
    turned_rows = pl.pallas_call(
        kernel,
        out_shape=jax.ShapeDtypeStruct((2048, 256), BF16),
        in_specs=[hbm, vmem, hbm, hbm, hbm],
        out_specs=hbm,
        scratch_shapes=[
            pltpu.VMEM((256, 512), BF16),
            pltpu.VMEM((4, 2, 16, 128), F32),
            pltpu.VMEM((4, 8, 64, 512), BF16),
            pltpu.VMEM((4, 16, 4, 16, 512), BF16),
            pltpu.VMEM((4, 16, 2, 2, 16, 512), BF16),
            pltpu.VMEM((4, 4, 2, 2, 2, 16, 512), BF16),
            pltpu.VMEM((4, 2, 128, 512), F32),
            pltpu.VMEM((2, 4, 2, 128, 512), BF16),
            pltpu.VMEM((2, 2048, 128), F32),
            pltpu.VMEM((64, 4, 16, 128), BF16),
            pltpu.VMEM((64, 4, 16, 128), BF16),
            pltpu.VMEM((4, 4, 2, 2, 32, 128), BF16),
            pltpu.VMEM((4, 4, 2, 32, 128), BF16),
            pltpu.VMEM((64, 4, 16, 128), BF16),
            pltpu.VMEM((64, 4, 16, 128), BF16),
            pltpu.VMEM((1024, 128), F32),
            pltpu.VMEM((2048, 256), BF16),
            pltpu.SemaphoreType.DMA((4,)),
            pltpu.SemaphoreType.DMA((2, KL)),
            pltpu.SemaphoreType.DMA((2, KL, 4)),
            pltpu.SemaphoreType.DMA((2, KL, 4)),
            pltpu.SemaphoreType.DMA((2, KL, 2)),
            pltpu.SemaphoreType.DMA((2, KL)),
            pltpu.SemaphoreType.DMA((2,)),
        ],
        compiler_params=pltpu.CompilerParams(
            collective_id=0, has_side_effects=True, vmem_limit_bytes=60 << 20
        ),
        cost_estimate=pl.CostEstimate(flops=2 * 10**9, bytes_accessed=16 << 20, transcendentals=0),
        name="tiles",
    )(
        cas,
        jnp.transpose(tile_ranks, (0, 2, 1)),
        traces,
        left_factors.reshape(4, 16, 2, 2, 16, 512),
        right_factors,
    )
    return pl.pallas_call(
        inverse,
        grid=(2, 8 // PART),
        out_shape=jax.ShapeDtypeStruct((4, 8, 64, 512), BF16),
        in_specs=[
            pl.BlockSpec((128 * PART, 256), lambda q, n: (q * (8 // PART) + n, 0)),
            pl.BlockSpec((256, 512), lambda q, n: (0, 0)),
        ],
        out_specs=pl.BlockSpec((2, PART, 64, 512), lambda q, n: (q, n, 0, 0)),
        cost_estimate=pl.CostEstimate(flops=2**29, bytes_accessed=3 << 20, transcendentals=0),
        name="inverse",
    )(turned_rows, hartley_rows(512, 256, KL))


def solution(mesh):
    in_specs = (
        P("col", "freq", None, None),
        P("freq", None, "col", None, None),
        P("freq", None, "col", None, None),
        P("freq", None, "col"),
    )
    out_specs = P("col", "freq", None, None)
    return jax.shard_map(shards, mesh=mesh, in_specs=in_specs, out_specs=out_specs, check_vma=False)
```

```python
import jax
import jax.numpy as jnp
import numpy as np
from jax import lax
from jax.experimental import pallas as pl
from jax.experimental.pallas import tpu as pltpu
from jax.sharding import PartitionSpec as P

MESH = pl.DeviceIdType.MESH
F32, BF16 = jnp.float32, jnp.bfloat16
NZ, NY, NC, NX = 8, 4, 2, 4
NFREQ = NZ * NY * NC
KL = 4
PART = 8


def hartley_rows(time_count, freq_count, stride=1):
    freqs = np.arange(freq_count).reshape(-1, stride).T.reshape(-1)
    phase = freqs[:, None] * np.arange(time_count)[None, :] % time_count
    angle = np.float32(2.0 * np.pi / time_count) * phase.astype(np.float32)
    table = (np.cos(angle) + np.sin(angle)) / np.sqrt(np.float32(time_count))
    return jnp.asarray(table.astype(np.float32)).astype(BF16)


def freq_peer(f, i):
    z, y, c = f // (NY * NC), lax.rem(f // NC, NY), lax.rem(f, NC)
    dz, dy, dc = lax.rem(i, NZ), lax.rem(i // NZ, NY), i // (NZ * NY)
    return (lax.rem(z + dz, NZ) * NY + lax.rem(y + dy, NY)) * NC + lax.rem(c + dc, NC)


def kernel(
    cas_in, ranks, traces, left, right, out,
    cas, limits, tr, rt, lloc, lrecv, hold, chain, stage, send, recv, csend, crecv, send2, recv2, stage2, turned_rows,
    local_sem, spec_sem, left_sem, coef_sem, chain_sem, syn_sem, out_sem,
):
    f, x = lax.axis_index("freq"), lax.axis_index("col")
    after, before, across = lax.rem(x + 1, NX), lax.rem(x + NX - 1, NX), lax.rem(x + 2, NX)
    routes = [(across, 0, after), (after, 1, after), (across, 1, before), (before, 0, before)]

    def spec_copy(i, k):
        d = freq_peer(f, i)
        return pltpu.make_async_remote_copy(
            send.at[d, k], recv.at[f, k], spec_sem.at[0, k], spec_sem.at[1, k],
            device_id=(d, x), device_id_type=MESH,
        )

    def syn_copy(i, k):
        d = freq_peer(f, i)
        return pltpu.make_async_remote_copy(
            send2.at[d, k], recv2.at[f, k], syn_sem.at[0, k], syn_sem.at[1, k],
            device_id=(d, x), device_id_type=MESH,
        )

    def left_copy(slot, k):
        owner, q, d = routes[slot]
        return pltpu.make_async_remote_copy(
            left.at[k, pl.ds(4 * owner + 2 * q, 2)], lrecv.at[k, slot],
            left_sem.at[0, k, slot], left_sem.at[1, k, slot],
            device_id=(f, d), device_id_type=MESH,
        )

    def coef_copy(slot, k):
        owner, q, d = routes[slot]
        return pltpu.make_async_remote_copy(
            csend.at[k, owner, q], crecv.at[k, slot],
            coef_sem.at[0, k, slot], coef_sem.at[1, k, slot],
            device_id=(f, d), device_id_type=MESH,
        )

    def chain_copy(q, k):
        return pltpu.make_async_remote_copy(
            chain.at[0, k, q], chain.at[1, k, q], chain_sem.at[0, k, q], chain_sem.at[1, k, q],
            device_id=(f, (after, before)[q]), device_id_type=MESH,
        )

    def whole(src, dst, sems, k):
        return pltpu.make_async_remote_copy(
            src, dst, sems.at[0, k], sems.at[1, k], device_id=(f, x), device_id_type=MESH
        )

    rest = pl.ds(0, NFREQ - 1)

    def spec_all(k):
        return whole(send.at[rest, k], recv.at[rest, k], spec_sem, k)

    def syn_all(k):
        return whole(send2.at[rest, k], recv2.at[rest, k], syn_sem, k)

    def far_left(k):
        left_copy(0, k).start()
        left_copy(2, k).start()

    def near_left(k):
        left_copy(1, k).start()
        left_copy(3, k).start()

    traces_in = pltpu.make_async_copy(traces, tr, local_sem.at[0])
    right_in = pltpu.make_async_copy(right, rt, local_sem.at[1])
    left_in = pltpu.make_async_copy(left, lloc, local_sem.at[2])
    cas_load = pltpu.make_async_copy(cas_in, cas, local_sem.at[3])
    traces_in.start()
    cas_load.start()
    right_in.start()
    left_in.start()

    barrier = pltpu.get_barrier_semaphore()

    def greet(i, carry):
        pl.semaphore_signal(
            barrier, inc=1, device_id=(freq_peer(f, i), x), device_id_type=MESH
        )
        return carry

    lax.fori_loop(1, NFREQ, greet, 0)
    for d in (after, before):
        pl.semaphore_signal(barrier, inc=1, device_id=(f, d), device_id_type=MESH)

    cas_load.wait()
    traces_in.wait()

    def spectra(n, carry):
        p, s = n // 4, 2 * lax.rem(n, 4)
        rows = jnp.concatenate(
            [tr[2 * p, s], tr[2 * p + 1, s], tr[2 * p, s + 1], tr[2 * p + 1, s + 1]], axis=0
        )
        acc = lax.dot_general(
            cas[...], rows, (((1,), (1,)), ((), ())), preferred_element_type=F32
        )
        stage[p, pl.ds(s, 256, 8), :] = acc[:, :128]
        stage[p, pl.ds(s + 1, 256, 8), :] = acc[:, 128:]
        return carry

    lax.fori_loop(0, 8, spectra, 0, unroll=2)

    def pack(n, carry):
        halves = [stage[p, pl.ds(n * 256, 256), :].reshape(8, KL, 8, 128) for p in range(2)]
        send[pl.ds(n * 8, 8)] = jnp.concatenate(halves, axis=2).astype(BF16)
        return carry

    lax.fori_loop(0, 8, pack, 0)

    row16 = lax.broadcasted_iota(jnp.int32, (16, 16), 0)
    diagonal = row16 == lax.broadcasted_iota(jnp.int32, (16, 16), 1)
    low_half = lax.broadcasted_iota(jnp.int32, (16, 128), 1) < 64
    for k in range(KL):
        for p in range(2):
            columns = [
                jnp.sum(
                    jnp.where(diagonal, ranks[k, 2 * p + b : 2 * p + b + 1].astype(F32), 0.0),
                    axis=1, keepdims=True,
                )
                for b in range(2)
            ]
            limits[k, p] = jnp.where(
                low_half, jnp.broadcast_to(columns[0], (16, 128)), jnp.broadcast_to(columns[1], (16, 128))
            )

    pl.semaphore_wait(barrier, NFREQ - 1 + 2)
    far_left(0)
    near_left(0)
    far_left(1)
    near_left(1)

    def start_spec(n, carry):
        k, i = n // NFREQ, lax.rem(n, NFREQ)

        @pl.when(i > 0)
        def _():
            spec_copy(i, k).start()

        return carry

    lax.fori_loop(0, KL * NFREQ, start_spec, 0)
    recv[pl.ds(f, 1)] = send[pl.ds(f, 1)]
    right_in.wait()

    lane = lax.broadcasted_iota(jnp.int32, (256, 128), 1)
    rank_index = lax.rem(lax.broadcasted_iota(jnp.int32, (256, 128), 0), 16).astype(F32)

    def coeffs(k):
        spec_all(k).wait_recv()
        spectrum = recv[:, k].astype(F32)
        for p in range(2):
            rows = spectrum[:, 8 * p : 8 * p + 8].reshape(512, 128).astype(BF16)
            products = [
                jnp.dot(rt[k, :, 2 * p + b].reshape(256, 512), rows, preferred_element_type=F32)
                for b in range(2)
            ]
            bound = jnp.concatenate(
                [jnp.broadcast_to(limits[k, p, r : r + 1], (16, 128)) for r in range(16)], axis=0
            )
            kept = jnp.where(lane < 64, products[0], products[1])
            kept = jnp.where(rank_index < bound, kept, 0.0).astype(BF16)
            csend[k, :, :, p] = kept.reshape(4, 2, 32, 128)
        for slot in (0, 2, 1, 3):
            coef_copy(slot, k).start()

    def spread(k, pairs):
        halves = [pair.T.reshape(64, 8, 128) for pair in pairs]
        send2[:, k] = jnp.concatenate(halves, axis=1).astype(BF16)
        recv2[pl.ds(f, 1), k] = send2[pl.ds(f, 1), k]

        def start(i, carry):
            syn_copy(i, k).start()
            return carry

        lax.fori_loop(1, NFREQ, start, 0)

    half = lax.broadcasted_iota(jnp.int32, (64, 256), 1) // 16 % 2

    def pair_sum(k, owner, q, slot):
        coefs = jnp.concatenate(
            [csend[k, owner, q].reshape(64, 128), crecv[k, slot].reshape(64, 128)], axis=0
        )
        turned = coefs.astype(F32).T
        lanes = jnp.concatenate([turned[:64], turned[64:]], axis=1)
        lhs = jnp.concatenate([jnp.where(half == r, lanes, 0.0) for r in range(2)], axis=0)
        rhs = []
        for b in range(2):
            rhs += [lloc[k, pl.ds(4 * owner + 2 * q, 2), p, b].reshape(32, 512) for p in range(2)]
            rhs += [lrecv[k, slot, :, p, b].reshape(32, 512) for p in range(2)]
        return jnp.dot(
            lhs.astype(BF16), jnp.concatenate(rhs, axis=0), preferred_element_type=F32
        )

    def arrived(k, slot):
        left_copy(slot, k).wait_recv()
        coef_copy(slot, k).wait_recv()

    def sums(k):
        arrived(k, 0)
        chain[0, k, 0] = pair_sum(k, after, 0, 0).astype(BF16)
        chain_copy(0, k).start()
        arrived(k, 2)
        chain[0, k, 1] = pair_sum(k, before, 1, 2).astype(BF16)
        chain_copy(1, k).start()

    def own_sums(k):
        arrived(k, 3)
        hold[k, 0] = pair_sum(k, x, 0, 3)
        arrived(k, 1)
        hold[k, 1] = pair_sum(k, x, 1, 1)

    def finish(k):
        for q in range(2):
            chain_copy(q, k).wait_recv()
        spread(k, [hold[k, q] + chain[1, k, q].astype(F32) for q in range(2)])

    steps = ["C0", "A2", "C1", "W", "X0", "B2", "Y0", "A3", "C2", "F0", "X1", "B3", "Y1", "C3", "F1", "X2", "X3", "Y2", "F2", "Y3", "F3"]
    for step in steps:
        if step == "W":
            left_in.wait()
            continue
        dict(C=coeffs, A=far_left, B=near_left, X=sums, Y=own_sums, F=finish)[step[0]](int(step[1]))

    def lanes_out(h):
        part = (slice(None), pl.ds(128 * h, 128))
        return pltpu.make_async_copy(turned_rows.at[part], out.at[part], out_sem.at[h])

    for k in range(KL):
        syn_all(k).wait_recv()
        stage2[...] = recv2[:, k].astype(F32).reshape(1024, 128)
        for n in range(16):
            turned_rows[128 * n : 128 * n + 128, 64 * k : 64 * k + 64] = (
                stage2[pl.ds(n, 64, 16), :].astype(BF16).T
            )

        if k % 2:
            lanes_out(k // 2).start()
    for k in range(KL):
        spec_all(k).wait_send()
        syn_all(k).wait_send()
        for slot in range(4):
            left_copy(slot, k).wait_send()
            coef_copy(slot, k).wait_send()
        for q in range(2):
            chain_copy(q, k).wait_send()
    for h in range(2):
        lanes_out(h).wait()


def inverse(rows, cas, out):
    acc = jnp.dot(rows[...], cas[...], preferred_element_type=F32).astype(BF16)
    for b in range(acc.shape[0] // 128):
        out[0, b] = acc[128 * b : 128 * b + 64]
        out[1, b] = acc[128 * b + 64 : 128 * b + 128]


def shards(traces, left_factors, right_factors, tile_ranks):
    cas = hartley_rows(512, 256)
    vmem = pl.BlockSpec(memory_space=pltpu.VMEM)
    hbm = pl.BlockSpec(memory_space=pl.ANY)
    turned_rows = pl.pallas_call(
        kernel,
        out_shape=jax.ShapeDtypeStruct((2048, 256), BF16),
        in_specs=[hbm, vmem, hbm, hbm, hbm],
        out_specs=hbm,
        scratch_shapes=[
            pltpu.VMEM((256, 512), BF16),
            pltpu.VMEM((4, 2, 16, 128), F32),
            pltpu.VMEM((4, 8, 64, 512), BF16),
            pltpu.VMEM((4, 16, 4, 16, 512), BF16),
            pltpu.VMEM((4, 16, 2, 2, 16, 512), BF16),
            pltpu.VMEM((4, 4, 2, 2, 2, 16, 512), BF16),
            pltpu.VMEM((4, 2, 128, 512), F32),
            pltpu.VMEM((2, 4, 2, 128, 512), BF16),
            pltpu.VMEM((2, 2048, 128), F32),
            pltpu.VMEM((64, 4, 16, 128), BF16),
            pltpu.VMEM((64, 4, 16, 128), BF16),
            pltpu.VMEM((4, 4, 2, 2, 32, 128), BF16),
            pltpu.VMEM((4, 4, 2, 32, 128), BF16),
            pltpu.VMEM((64, 4, 16, 128), BF16),
            pltpu.VMEM((64, 4, 16, 128), BF16),
            pltpu.VMEM((1024, 128), F32),
            pltpu.VMEM((2048, 256), BF16),
            pltpu.SemaphoreType.DMA((4,)),
            pltpu.SemaphoreType.DMA((2, KL)),
            pltpu.SemaphoreType.DMA((2, KL, 4)),
            pltpu.SemaphoreType.DMA((2, KL, 4)),
            pltpu.SemaphoreType.DMA((2, KL, 2)),
            pltpu.SemaphoreType.DMA((2, KL)),
            pltpu.SemaphoreType.DMA((2,)),
        ],
        compiler_params=pltpu.CompilerParams(
            collective_id=0, has_side_effects=True, vmem_limit_bytes=60 << 20
        ),
        cost_estimate=pl.CostEstimate(flops=2 * 10**9, bytes_accessed=16 << 20, transcendentals=0),
        name="tiles",
    )(
        cas,
        jnp.transpose(tile_ranks, (0, 2, 1)),
        traces,
        left_factors.reshape(4, 16, 2, 2, 16, 512),
        right_factors,
    )
    return pl.pallas_call(
        inverse,
        grid=(2, 8 // PART),
        out_shape=jax.ShapeDtypeStruct((4, 8, 64, 512), BF16),
        in_specs=[
            pl.BlockSpec((128 * PART, 256), lambda q, n: (q * (8 // PART) + n, 0)),
            pl.BlockSpec((256, 512), lambda q, n: (0, 0)),
        ],
        out_specs=pl.BlockSpec((2, PART, 64, 512), lambda q, n: (q, n, 0, 0)),
        cost_estimate=pl.CostEstimate(flops=2**29, bytes_accessed=3 << 20, transcendentals=0),
        name="inverse",
    )(turned_rows, hartley_rows(512, 256, KL))


def solution(mesh):
    in_specs = (
        P("col", "freq", None, None),
        P("freq", None, "col", None, None),
        P("freq", None, "col", None, None),
        P("freq", None, "col"),
    )
    out_specs = P("col", "freq", None, None)
    return jax.shard_map(shards, mesh=mesh, in_specs=in_specs, out_specs=out_specs, check_vma=False)
```
